256 devices in a mesh: down: 8 (over z), cross: 16 (over y, x), elev: 2 (over core).
Axes of the slice: x: 4, y: 4, z: 8, core: 2. Of those that a mesh axis runs over, the one named last changes fastest.
Arguments:
- source: float32 [256, 32, 256], P(('cross', 'elev'), 'down'), may hold values from -2 to 2
- pivot_inverse: bfloat16 [256, 32, 256, 256], P(('cross', 'elev'), 'down'), may hold values from -1.1 to 1.2
- coupling: bfloat16 [256, 32, 256, 256], P(('cross', 'elev'), 'down'), may hold values from -1.1 to 1.2
- skeleton_map: bfloat16 [256, 256, 256], P(('cross', 'elev')), may hold values from -0.375 to 0.375
- owners: int32 [256, 32], P(('cross', 'elev'), 'down'), may hold values from 0 to 255
Outputs:
- pressure: float32 [256, 32, 256], P(('cross', 'elev'), 'down')
- forces: float32 [256, 32, 256], P(('cross', 'elev'), 'down')
The draws below stay inside these ranges and needn't reach their ends.
All inputs are finite; a program needn't handle non-finite values.
Results may differ from the reference program's by a relative error of at most 0.0003.
Values sent between devices are 32-bit elements; how exact they have to be, the bound alone decides.
No kernel may reach another device: no remote copies, remote signals or barrier semaphores. Data moves between devices by JAX's collectives and lax.ppermute only.
A program may use at most 128 MiB of HBM per device.

```python
import jax
import jax.numpy as jnp
from jax import lax

B = 256
LINE_COUNT = 256
BLOCKS_PER_LINE = 32
TARGETS = 256


noise_scale = 0.0125


def rough_part(key, shape):
    return noise_scale * jnp.clip(jax.random.normal(key, shape, jnp.float32), -4.0, 4.0)


def draw_pivot_inverse(key, part):
    first_key = jax.random.fold_in(key, 11)
    second_key = jax.random.fold_in(key, 12)
    lower_end = 0.9
    upper_end = 1.1
    diagonal = jax.random.uniform(first_key, (LINE_COUNT, BLOCKS_PER_LINE, B), jnp.float32, lower_end, upper_end)
    identity = jnp.eye(B, dtype=jnp.float32)
    matrix = rough_part(second_key, (LINE_COUNT, BLOCKS_PER_LINE, B, B)) + identity * diagonal[..., None]
    return matrix.astype(jnp.bfloat16)


def draw_coupling(key, part):
    first_key = jax.random.fold_in(key, 21)
    second_key = jax.random.fold_in(key, 22)
    third_key = jax.random.fold_in(key, 23)
    key_number_four = jax.random.fold_in(key, 24)
    fifth_key = jax.random.fold_in(key, 25)
    share = 0.5
    quick_mask = jax.random.bernoulli(first_key, share, (LINE_COUNT, 1, B))
    quick_rate = jax.random.uniform(second_key, (LINE_COUNT, 1, B), jnp.float32, 0.2, 0.6)
    gradual_rate = 0.25 ** (1.0 / BLOCKS_PER_LINE) * jax.random.uniform(third_key, (LINE_COUNT, BLOCKS_PER_LINE, B), jnp.float32, 0.985, 1.015)
    spike_mask = jax.random.bernoulli(key_number_four, 2.0 / BLOCKS_PER_LINE, (LINE_COUNT, BLOCKS_PER_LINE, 1))
    damping_rate = jnp.where(quick_mask, quick_rate, gradual_rate) * jnp.where(spike_mask, 0.6, 1.0)
    identity = jnp.eye(B, dtype=jnp.float32)
    matrix = rough_part(fifth_key, (LINE_COUNT, BLOCKS_PER_LINE, B, B)) - identity * damping_rate[..., None]
    return matrix.astype(jnp.bfloat16)


def touch_ends(array, rng, least, largest):
    place = [jax.random.randint(jax.random.fold_in(rng, axis), (), 0, length) for axis, length in enumerate(array.shape)]
    longest = array.shape.index(max(array.shape))
    beside = place[:longest] + [(place[longest] + 1) % array.shape[longest]] + place[longest + 1:]
    return array.at[tuple(place)].set(least).at[tuple(beside)].set(largest)


def shard_levels(stream_key, dims, pieces, low, largest):
    gain, own = 1.0, jax.random.fold_in(stream_key, 6)
    for dim, shards_of in pieces:
        draws = jnp.exp(jax.random.uniform(jax.random.fold_in(own, dim), (shards_of,), jnp.float32, low / len(pieces), largest / len(pieces)))
        gain = gain * jnp.repeat(draws, dims[dim] // shards_of).reshape([-1 if axis == dim else 1 for axis in range(len(dims))])
    return gain


def noise(stream_key, shape, deviation, most, cuts=(), kind=jnp.bfloat16):
    factor_of = shard_levels(stream_key, shape, cuts, -0.22, 0.18) if cuts else 1.0
    array = jax.random.normal(stream_key, shape, jnp.float32) * deviation * factor_of
    return jnp.minimum(jnp.maximum(array, -most), most).astype(kind)


def setup_inputs(seed: int = 0) -> dict:
    streams_of = jax.random.split(jax.random.key(seed), 6)
    return {
        "source": noise(streams_of[0], (LINE_COUNT, BLOCKS_PER_LINE, B), 0.3, 2.0, ((0, 32), (1, 8)), jnp.float32),
        "pivot_inverse": draw_pivot_inverse(jax.random.fold_in(streams_of[5], 71), 0),
        "coupling": draw_coupling(jax.random.fold_in(streams_of[5], 71), 0),
        "skeleton_map": noise(streams_of[3], (LINE_COUNT, B, B), B ** -0.5, 0.375, ((0, 32),)),
        "owners": touch_ends(jax.random.randint(streams_of[4], (LINE_COUNT, BLOCKS_PER_LINE), 0, TARGETS), jax.random.fold_in(streams_of[4], 1), 0, TARGETS - 1).astype(jnp.int32),
    }


highest = lax.Precision.HIGHEST


def apply_block(matrix, vector):
    return jnp.einsum("nab,nb->na", matrix.astype(jnp.float32), vector, precision=highest)


def apply_transposed(matrix, vector):
    return jnp.einsum("nba,nb->na", matrix.astype(jnp.float32), vector, precision=highest)


def reference(source, pivot_inverse, coupling, skeleton_map, owners):
    columns = jnp.arange(BLOCKS_PER_LINE, dtype=jnp.int32)

    def advance(carried, column):
        pivot = lax.dynamic_index_in_dim(pivot_inverse, column, 1, keepdims=False)
        lower = lax.dynamic_index_in_dim(coupling, column, 1, keepdims=False)
        given = lax.dynamic_index_in_dim(source, column, 1, keepdims=False)
        result = apply_block(pivot, given - apply_block(lower, carried))
        return result, result

    start = jnp.zeros((LINE_COUNT, B), jnp.float32)
    leftover, forward = lax.scan(advance, start, columns)

    def retreat(carried, column):
        pivot = lax.dynamic_index_in_dim(pivot_inverse, column, 1, keepdims=False)
        lower = lax.dynamic_index_in_dim(coupling, column, 1, keepdims=False)
        value = lax.dynamic_index_in_dim(forward, column, 0, keepdims=False) - apply_block(pivot, carried)
        return apply_transposed(lower, value), value

    remainder, values = lax.scan(retreat, start, columns, reverse=True)
    pressure = jnp.swapaxes(values, 0, 1)
    line_force = jnp.einsum("nab,njb->nja", skeleton_map.astype(jnp.float32), pressure, precision=highest)
    slots = jnp.arange(TARGETS, dtype=jnp.int32)
    onehot = (owners[:, :, None] == slots[None, None, :]).astype(jnp.float32)
    forces = jnp.einsum("njt,njb->tjb", onehot, line_force, precision=highest)
    return pressure, forces
```

```python
import functools

import jax
import jax.numpy as jnp
from jax import lax
from jax.experimental import pallas as pl
from jax.experimental.pallas import tpu as pltpu
from jax.sharding import PartitionSpec as P

F32 = jnp.float32
BF16 = jnp.bfloat16
PLANE = ("cross", "elev")
MIB = 1024 * 1024
IN_VMEM = pl.BlockSpec(memory_space=pltpu.VMEM)
IN_HBM = pl.BlockSpec(memory_space=pltpu.HBM)
ANYWHERE = pl.BlockSpec(memory_space=pl.ANY)


def times(rows, matrix, transposed):
    return lax.dot_general(
        rows, matrix, (((1,), (1 if transposed else 0,)), ((), ())), preferred_element_type=F32
    )


def spread(vector):
    high = vector.astype(BF16).astype(F32)
    rest = vector - high
    middle = rest.astype(BF16).astype(F32)
    low = rest - middle
    parts = [high, middle, low]
    if vector.shape[0] % 16:
        parts.append(jnp.zeros_like(low))
    return jnp.concatenate(parts, axis=0).astype(BF16)


def per_line(vector, matrix_of, transposed, lines, twice=False):
    count = vector.shape[0]
    rows = spread(vector)
    if twice:
        rows = jnp.concatenate([rows, rows], axis=1)
    line_of = lax.rem(lax.broadcasted_iota(jnp.int32, vector.shape, 0), lines)
    total = jnp.zeros_like(vector)
    for line in range(lines):
        product = times(rows, matrix_of(line), transposed)
        product = product[:count] + product[count : 2 * count] + product[2 * count : 3 * count]
        total = jnp.where(line_of == line, product, total)
    return total


def halves(matrix):
    high = matrix.astype(BF16)
    low = (matrix - high.astype(F32)).astype(BF16)
    return jnp.concatenate([high, low], axis=1)


def product_of(pair, matrix, transposed):
    return times(pair, jnp.concatenate([matrix, matrix], axis=1 if transposed else 0), transposed)


def unit(size, sign=1.0):
    across = lax.broadcasted_iota(jnp.int32, (size, size), 0)
    along = lax.broadcasted_iota(jnp.int32, (size, size), 1)
    return jnp.where(across == along, sign, 0.0).astype(BF16)


def first_sweep(source, pivots, couple, leaving, pivots_here, couple_here, semaphores):
    lines, columns = source.shape[:2]

    @pl.when(lax.axis_index("down") == 0)
    def _():
        def fetch(column, far, near, kind):
            return pltpu.make_async_copy(far.at[:, column], near.at[:, column], semaphores.at[2 * column + kind])

        copies = [fetch(0, pivots, pivots_here, 1)]
        for column in range(1, columns):
            copies.append(fetch(column, couple, couple_here, 0))
            copies.append(fetch(column, pivots, pivots_here, 1))
        ahead = 4
        for copy in copies[:ahead]:
            copy.start()

        def take(at):
            copies[at].wait()
            if at + ahead < len(copies):
                copies[at + ahead].start()

        carried = None
        for column in range(columns):
            given = source[:, column, :]
            if column:
                take(2 * column - 1)
                given = given - per_line(carried, lambda l: couple_here[l, column], True, lines)
            take(2 * column)
            carried = per_line(given, lambda l: pivots_here[l, column], True, lines)
        leaving[...] = carried


EXTRA = 16
TOGETHER = 4


def store_pair(matrix, line, pair):
    size = matrix.shape[2]
    matrix[line, :size] = pair[:, :size]
    matrix[line, size:] = pair[:, size:]


def forward_rows(source, pivots, couple, lines, keep=None):
    columns, size = pivots.shape[1], pivots.shape[2]
    blank = jnp.zeros((EXTRA - 1, size), F32)
    values = None
    for column in range(columns):
        given = []
        for at, line in enumerate(lines):
            own = jnp.concatenate([source[line, pl.ds(column, 1), :], blank], axis=0)
            if column:
                sent = product_of(halves(values[at]), couple[line, column], True)
                given.append(jnp.concatenate([-sent[:size], own - sent[size:]], axis=0))
            else:
                given.append(jnp.concatenate([-times(unit(size), couple[line, 0], True), own], axis=0))
        values = [product_of(halves(x), pivots[l, column], True) for x, l in zip(given, lines)]
        if keep is not None and column < columns - 1:
            for at, value in enumerate(values):
                keep[at, column] = value
    return values


def transfer(source, pivots_far, couple_far, matrix, base, pivots, couple, kept, semaphores):
    lines, columns = pivots.shape[:2]
    size = pivots.shape[2]
    here = lax.axis_index("down")
    last = lax.axis_size("down") - 1

    def fetch(line, act):
        for kind, (far, near) in enumerate(((couple_far, couple), (pivots_far, pivots))):
            act(pltpu.make_async_copy(far.at[line], near.at[line], semaphores.at[kind, line]))

    def arrive(some, first):
        for line in some:
            fetch(line, lambda copy: copy.wait())

        @pl.when(first + TOGETHER < lines)
        def _():
            for line in some:
                fetch(line + TOGETHER, lambda copy: copy.start())

    def hand_over(some, values):
        for line, value in zip(some, values):
            store_pair(matrix, line, halves(value[:size]))
            base[pl.ds(line, 1), :] = value[size : size + 1]

    @pl.when(here > 0)
    def _():
        for line in range(TOGETHER):
            fetch(line, lambda copy: copy.start())

    @pl.when(jnp.logical_and(here > 0, here < last))
    def _():
        @pl.loop(0, lines, step=TOGETHER)
        def _(first):
            some = [first + k for k in range(TOGETHER)]
            arrive(some, first)
            hand_over(some, forward_rows(source, pivots, couple, some))

    @pl.when(here == last)
    def _():
        @pl.loop(0, lines, step=TOGETHER)
        def _(first):
            some = [first + k for k in range(TOGETHER)]
            arrive(some, first)
            values = forward_rows(source, pivots, couple, some, kept)
            for column in range(columns - 1, -1, -1):
                values = [product_of(halves(x), couple[l, column], False) for x, l in zip(values, some)]
                if column:
                    values = [
                        kept[at, column - 1] - product_of(halves(x), pivots[l, column - 1], True)
                        for at, (x, l) in enumerate(zip(values, some))
                    ]
            hand_over(some, values)


def reverse_transfer(pivots, couple, _, matrix):
    lines, columns = pivots.shape[:2]
    size = pivots.shape[2]
    here = lax.axis_index("down")
    last = lax.axis_size("down") - 1

    @pl.when(jnp.logical_and(here > 0, here < last))
    def _():
        @pl.loop(0, lines, step=TOGETHER)
        def _(first):
            some = [first + k for k in range(TOGETHER)]
            pairs = [times(unit(size, -1.0), pivots[l, columns - 1], True).astype(BF16) for l in some]
            for column in range(columns - 1, -1, -1):
                if column == columns - 1:
                    values = [times(x, couple[l, column], False) for x, l in zip(pairs, some)]
                else:
                    values = [product_of(x, couple[l, column], False) for x, l in zip(pairs, some)]
                pairs = [halves(value) for value in values]
                if column:
                    pairs = [halves(-product_of(x, pivots[l, column - 1], True)) for x, l in zip(pairs, some)]
            for line, pair in zip(some, pairs):
                store_pair(matrix, line, pair)


def step(place, arrived, matrix, base, _, out):
    lines = base.shape[0]

    @pl.when(lax.axis_index("down") == place)
    def _():
        out[...] = base[...] + per_line(arrived[...], lambda l: matrix[l], False, lines, twice=True)


def own_part(pivots, couple, source, arrived, _, forward, base):
    lines, columns = pivots.shape[:2]
    carried = jnp.sum(arrived[...], axis=0)
    for column in range(columns):
        given = source[:, column, :] - per_line(carried, lambda l: couple[l, column], True, lines)
        carried = per_line(given, lambda l: pivots[l, column], True, lines)
        forward[column] = carried
    value = carried
    for column in range(columns - 1, -1, -1):
        carried = per_line(value, lambda l: couple[l, column], False, lines)
        if column:
            value = forward[column - 1] - per_line(carried, lambda l: pivots[l, column - 1], True, lines)
    base[...] = carried


def finish(pivots, couple, skeleton, codes, forward, arrived, pressure, pushed):
    lines, columns = pivots.shape[:2]
    carried = jnp.sum(arrived[...], axis=0)
    values = [None] * columns
    for column in range(columns - 1, -1, -1):
        value = forward[column] - per_line(carried, lambda l: pivots[l, column], True, lines)
        values[column] = value
        pressure[:, column, :] = value
        if column:
            carried = per_line(value, lambda l: couple[l, column], False, lines)
    rows = columns * lines
    pushed[:rows] = per_line(jnp.concatenate(values, axis=0), lambda l: skeleton[l], True, lines)
    pushed[rows:] = codes[...]


def gather_rows(lines, columns, sides, *refs):
    blocks, outs = refs[: -sides], refs[-sides:]
    rows = lines * columns
    across, up = lax.axis_index("cross"), lax.axis_index("elev")
    width = blocks[0].shape[1]
    block_of = lax.broadcasted_iota(jnp.int32, (1, width), 1) // rows
    codes = jnp.zeros((1, width), F32)
    for at, block in enumerate(blocks):
        codes = jnp.where(block_of == at, block[rows : rows + 1, :], codes)
    values = jnp.concatenate([block[:rows, :] for block in blocks], axis=0)
    high = values.astype(BF16)
    rest = values - high.astype(F32)
    middle = rest.astype(BF16)
    low = (rest - middle.astype(F32)).astype(BF16)
    here = lax.broadcasted_iota(jnp.int32, (rows, 1), 0)
    wanted = []
    for way in range(sides):
        chip = (across // sides ^ way) * sides + lax.rem(across, sides)
        wanted.append((chip * 2 + up) * rows + here)
    wanted = jnp.concatenate(wanted, axis=0).astype(F32)
    chosen = jnp.where(wanted == codes, 1.0, 0.0).astype(BF16)
    total = times(chosen, high, False) + (times(chosen, middle, False) + times(chosen, low, False))
    for way in range(sides):
        outs[way][...] = total[way * rows : (way + 1) * rows]


def add_up(columns, *refs):
    parts, out = refs[:-1], refs[-1]
    total = parts[0][...]
    for part in parts[1:]:
        total = total + part[...]
    for row in range(out.shape[0]):
        out[row] = total[row * columns : (row + 1) * columns]


def call(body, out_shape, in_specs, scratch=(), name=None, limit=16):
    return pl.pallas_call(
        body,
        out_shape=out_shape,
        in_specs=in_specs,
        out_specs=jax.tree.map(lambda _: IN_VMEM, out_shape),
        scratch_shapes=list(scratch),
        compiler_params=pltpu.CompilerParams(vmem_limit_bytes=limit * MIB),
        name=name,
    )


def shaped(shape, dtype=F32):
    return jax.ShapeDtypeStruct(shape, dtype)


def shards(source, pivot_inverse, coupling, skeleton_map, owners):
    lines, columns, size = source.shape
    depth = lax.axis_size("down")
    vectors = shaped((lines, size))
    every = shaped((columns, lines, size))
    stacked = shaped((lines, 2 * size, size), BF16)

    matrices = pltpu.VMEM(pivot_inverse.shape, BF16)
    sent = call(
        first_sweep,
        vectors,
        [IN_VMEM, IN_HBM, IN_HBM],
        [matrices, matrices, pltpu.SemaphoreType.DMA((2 * columns,))],
        name="first_sweep",
        limit=51,
    )(source, pivot_inverse, coupling)
    arrivals = []
    base = matrix = back = None

    def advance(place, *operands):
        return call(
            functools.partial(step, place), vectors, [IN_VMEM, IN_VMEM, IN_VMEM, ANYWHERE], name="step"
        )(*operands)

    for hop in range(1, depth):
        arrived = lax.ppermute(sent, "down", [(hop - 1, hop)])
        arrivals.append(arrived)
        if hop == 1:
            matrix, base = call(
                transfer,
                (stacked, vectors),
                [IN_VMEM, IN_HBM, IN_HBM],
                [
                    matrices,
                    matrices,
                    pltpu.VMEM((TOGETHER, columns - 1, size + EXTRA, size), F32),
                    pltpu.SemaphoreType.DMA((2, lines)),
                ],
                name="transfer",
                limit=49,
            )(source, pivot_inverse, coupling)
        if hop == 4:
            back = call(
                reverse_transfer, stacked, [IN_VMEM, IN_VMEM, ANYWHERE], name="reverse_transfer"
            )(pivot_inverse, coupling, sent)
        sent = advance(hop, arrived, matrix, base, base if back is None else back)
    forward, base = call(
        own_part, (every, vectors), [IN_VMEM] * 4 + [ANYWHERE], name="own_part"
    )(pivot_inverse, coupling, source, jnp.stack(arrivals), sent)
    arrivals = []
    for hop in range(depth - 1, 0, -1):
        arrived = lax.ppermute(sent, "down", [(hop, hop - 1)])
        arrivals.append(arrived)
        if hop > 1:
            sent = advance(hop - 1, arrived, back, base, base)
    rows = lines * columns
    codes = (owners * columns + jnp.arange(columns, dtype=jnp.int32)).T.reshape(1, rows).astype(F32)
    codes = jnp.broadcast_to(jnp.tile(codes, (1, size // rows)), (8, size))
    pressure, own = call(
        finish, (shaped(source.shape), shaped((rows + 8, size))), [IN_VMEM] * 6, name="finish"
    )(pivot_inverse, coupling, skeleton_map, codes, forward, jnp.stack(arrivals))
    chips = lax.axis_size("cross")
    sides = 4
    blocks = [own]
    for way in range(1, sides):
        blocks.append(lax.ppermute(own, "cross", [(chip, chip ^ way) for chip in range(chips)]))
    blocks += [lax.ppermute(block, "elev", [(0, 1), (1, 0)]) for block in blocks]
    parts = call(
        functools.partial(gather_rows, lines, columns, sides),
        (shaped((rows, size)),) * sides,
        [IN_VMEM] * len(blocks),
        name="gather_rows",
    )(*blocks)
    parts = [
        lax.ppermute(part, "cross", [(chip, chip ^ sides * way) for chip in range(chips)]) if way else part
        for way, part in enumerate(parts)
    ]
    forces = call(
        functools.partial(add_up, columns), shaped(source.shape), [IN_VMEM] * sides, name="add_up"
    )(*parts)
    return (pressure, forces)


def solution(mesh):
    in_specs = (
        P(PLANE, "down", None),
        P(PLANE, "down", None, None),
        P(PLANE, "down", None, None),
        P(PLANE, None, None),
        P(PLANE, "down"),
    )
    out_specs = (P(PLANE, "down", None), P(PLANE, "down", None))
    return jax.shard_map(shards, mesh=mesh, in_specs=in_specs, out_specs=out_specs, check_vma=False)
```

```python
import functools

import jax
import jax.numpy as jnp
from jax import lax
from jax.experimental import pallas as pl
from jax.experimental.pallas import tpu as pltpu
from jax.sharding import PartitionSpec as P

F32 = jnp.float32
BF16 = jnp.bfloat16
PLANE = ("cross", "elev")
MIB = 1024 * 1024
IN_VMEM = pl.BlockSpec(memory_space=pltpu.VMEM)
IN_HBM = pl.BlockSpec(memory_space=pltpu.HBM)
ANYWHERE = pl.BlockSpec(memory_space=pl.ANY)


def times(rows, matrix, transposed):
    return lax.dot_general(
        rows, matrix, (((1,), (1 if transposed else 0,)), ((), ())), preferred_element_type=F32
    )


def spread(vector):
    high = vector.astype(BF16).astype(F32)
    rest = vector - high
    middle = rest.astype(BF16).astype(F32)
    low = rest - middle
    parts = [high, middle, low]
    if vector.shape[0] % 16:
        parts.append(jnp.zeros_like(low))
    return jnp.concatenate(parts, axis=0).astype(BF16)


def per_line(vector, matrix_of, transposed, lines, twice=False):
    count = vector.shape[0]
    rows = spread(vector)
    if twice:
        rows = jnp.concatenate([rows, rows], axis=1)
    line_of = lax.rem(lax.broadcasted_iota(jnp.int32, vector.shape, 0), lines)
    total = jnp.zeros_like(vector)
    for line in range(lines):
        product = times(rows, matrix_of(line), transposed)
        product = product[:count] + product[count : 2 * count] + product[2 * count : 3 * count]
        total = jnp.where(line_of == line, product, total)
    return total


def halves(matrix):
    high = matrix.astype(BF16)
    low = (matrix - high.astype(F32)).astype(BF16)
    return jnp.concatenate([high, low], axis=1)


def product_of(pair, matrix, transposed):
    return times(pair, jnp.concatenate([matrix, matrix], axis=1 if transposed else 0), transposed)


def unit(size, sign=1.0):
    across = lax.broadcasted_iota(jnp.int32, (size, size), 0)
    along = lax.broadcasted_iota(jnp.int32, (size, size), 1)
    return jnp.where(across == along, sign, 0.0).astype(BF16)


def first_sweep(source_far, pivots, couple, leaving, source, pivots_here, couple_here, semaphores):
    lines, columns = source.shape[:2]

    @pl.when(lax.axis_index("down") == 0)
    def _():
        def fetch(column, far, near, kind):
            return pltpu.make_async_copy(far.at[:, column], near.at[:, column], semaphores.at[2 * column + kind])

        copies = [fetch(0, pivots, pivots_here, 1)]
        for column in range(1, columns):
            copies.append(fetch(column, couple, couple_here, 0))
            copies.append(fetch(column, pivots, pivots_here, 1))
        ahead = 4
        given_copy = pltpu.make_async_copy(source_far, source, semaphores.at[0])
        given_copy.start()
        for copy in copies[:ahead]:
            copy.start()
        given_copy.wait()

        def take(at):
            copies[at].wait()
            if at + ahead < len(copies):
                copies[at + ahead].start()

        carried = None
        for column in range(columns):
            given = source[:, column, :]
            if column:
                take(2 * column - 1)
                given = given - per_line(carried, lambda l: couple_here[l, column], True, lines)
            take(2 * column)
            carried = per_line(given, lambda l: pivots_here[l, column], True, lines)
        leaving[...] = carried


EXTRA = 16
TOGETHER = 4


def store_pair(matrix, line, pair):
    size = matrix.shape[2]
    matrix[line, :size] = pair[:, :size]
    matrix[line, size:] = pair[:, size:]


def forward_rows(source, pivots, couple, lines, keep=None):
    columns, size = pivots.shape[1], pivots.shape[2]
    blank = jnp.zeros((EXTRA - 1, size), F32)
    values = None
    for column in range(columns):
        given = []
        for at, line in enumerate(lines):
            own = jnp.concatenate([source[line, pl.ds(column, 1), :], blank], axis=0)
            if column:
                sent = product_of(halves(values[at]), couple[line, column], True)
                given.append(jnp.concatenate([-sent[:size], own - sent[size:]], axis=0))
            else:
                given.append(jnp.concatenate([-times(unit(size), couple[line, 0], True), own], axis=0))
        values = [product_of(halves(x), pivots[l, column], True) for x, l in zip(given, lines)]
        if keep is not None and column < columns - 1:
            for at, value in enumerate(values):
                keep[at, column] = value
    return values


def transfer(source, pivots_far, couple_far, matrix, base, pivots, couple, kept, semaphores):
    lines, columns = pivots.shape[:2]
    size = pivots.shape[2]
    here = lax.axis_index("down")
    last = lax.axis_size("down") - 1

    def fetch(line, act):
        for kind, (far, near) in enumerate(((couple_far, couple), (pivots_far, pivots))):
            act(pltpu.make_async_copy(far.at[line], near.at[line], semaphores.at[kind, line]))

    def arrive(some, first):
        for line in some:
            fetch(line, lambda copy: copy.wait())

        @pl.when(first + TOGETHER < lines)
        def _():
            for line in some:
                fetch(line + TOGETHER, lambda copy: copy.start())

    def hand_over(some, values):
        for line, value in zip(some, values):
            store_pair(matrix, line, halves(value[:size]))
            base[pl.ds(line, 1), :] = value[size : size + 1]

    @pl.when(here > 0)
    def _():
        for line in range(TOGETHER):
            fetch(line, lambda copy: copy.start())

    @pl.when(jnp.logical_and(here > 0, here < last))
    def _():
        @pl.loop(0, lines, step=TOGETHER)
        def _(first):
            some = [first + k for k in range(TOGETHER)]
            arrive(some, first)
            hand_over(some, forward_rows(source, pivots, couple, some))

    @pl.when(here == last)
    def _():
        @pl.loop(0, lines, step=TOGETHER)
        def _(first):
            some = [first + k for k in range(TOGETHER)]
            arrive(some, first)
            values = forward_rows(source, pivots, couple, some, kept)
            for column in range(columns - 1, -1, -1):
                values = [product_of(halves(x), couple[l, column], False) for x, l in zip(values, some)]
                if column:
                    values = [
                        kept[at, column - 1] - product_of(halves(x), pivots[l, column - 1], True)
                        for at, (x, l) in enumerate(zip(values, some))
                    ]
            hand_over(some, values)


def reverse_transfer(pivots, couple, _, matrix):
    lines, columns = pivots.shape[:2]
    size = pivots.shape[2]
    here = lax.axis_index("down")
    last = lax.axis_size("down") - 1

    @pl.when(jnp.logical_and(here > 0, here < last))
    def _():
        @pl.loop(0, lines, step=TOGETHER)
        def _(first):
            some = [first + k for k in range(TOGETHER)]
            pairs = [times(unit(size, -1.0), pivots[l, columns - 1], True).astype(BF16) for l in some]
            for column in range(columns - 1, -1, -1):
                if column == columns - 1:
                    values = [times(x, couple[l, column], False) for x, l in zip(pairs, some)]
                else:
                    values = [product_of(x, couple[l, column], False) for x, l in zip(pairs, some)]
                pairs = [halves(value) for value in values]
                if column:
                    pairs = [halves(-product_of(x, pivots[l, column - 1], True)) for x, l in zip(pairs, some)]
            for line, pair in zip(some, pairs):
                store_pair(matrix, line, pair)


def step(place, arrived, matrix, base, _, out):
    lines = base.shape[0]

    @pl.when(lax.axis_index("down") == place)
    def _():
        out[...] = base[...] + per_line(arrived[...], lambda l: matrix[l], False, lines, twice=True)


def own_part(pivots, couple, source, arrived, _, forward, base):
    lines, columns = pivots.shape[:2]
    carried = jnp.sum(arrived[...], axis=0)
    for column in range(columns):
        given = source[:, column, :] - per_line(carried, lambda l: couple[l, column], True, lines)
        carried = per_line(given, lambda l: pivots[l, column], True, lines)
        forward[column] = carried
    value = carried
    for column in range(columns - 1, -1, -1):
        carried = per_line(value, lambda l: couple[l, column], False, lines)
        if column:
            value = forward[column - 1] - per_line(carried, lambda l: pivots[l, column - 1], True, lines)
    base[...] = carried


def finish(pivots, couple, skeleton, codes, slots, forward, arrived, _, pressure, pushed, packed):
    lines, columns = pivots.shape[:2]
    carried = jnp.sum(arrived[...], axis=0)
    values = [None] * columns
    for column in range(columns - 1, -1, -1):
        value = forward[column] - per_line(carried, lambda l: pivots[l, column], True, lines)
        values[column] = value
        pressure[:, column, :] = value
        if column:
            carried = per_line(value, lambda l: couple[l, column], False, lines)
    rows = columns * lines
    force = per_line(jnp.concatenate(values, axis=0), lambda l: skeleton[l], True, lines)
    pushed[:rows] = force
    pushed[rows:] = codes[...]
    slot = lax.broadcasted_iota(jnp.int32, (packed.shape[0], rows), 0).astype(F32)
    chosen = jnp.where(slot == slots[:1, :rows], 1.0, 0.0).astype(BF16)
    parts = spread(force)
    packed[...] = times(chosen, parts[:rows], False) + (
        times(chosen, parts[rows : 2 * rows], False) + times(chosen, parts[2 * rows :], False)
    )


def gather_rows(lines, columns, sides, own, pair, across, mine, theirs):
    rows = lines * columns
    chip, core = lax.axis_index("cross"), lax.axis_index("elev")
    height = own.shape[0]
    blocks = [own[...], pair[:height], pair[height:], across[...]]
    block_of = lax.broadcasted_iota(jnp.int32, (1, len(blocks) * rows), 1) // rows
    codes = jnp.zeros(block_of.shape, F32)
    for at, block in enumerate(blocks):
        codes = jnp.where(block_of == at, block[rows : rows + 1, : len(blocks) * rows], codes)
    values = jnp.concatenate([block[:rows] for block in blocks], axis=0)
    high = values.astype(BF16)
    rest = values - high.astype(F32)
    middle = rest.astype(BF16)
    low = (rest - middle.astype(F32)).astype(BF16)
    here = lax.broadcasted_iota(jnp.int32, (rows, 1), 0)
    wanted = []
    for turn in range(2):
        holder = core if turn == 0 else 1 - core
        beside = 1 + 2 * holder
        for way, owner in ((0, holder), (2, holder), (beside, holder), (beside, 1 - holder)):
            target = (chip // sides ^ way) * sides + lax.rem(chip, sides)
            wanted.append((target * 2 + owner) * rows + here)
    wanted = jnp.concatenate(wanted, axis=0).astype(F32)
    chosen = jnp.where(wanted == codes, 1.0, 0.0).astype(BF16)
    total = times(chosen, high, False) + (times(chosen, middle, False) + times(chosen, low, False))
    mine[...] = total[: 4 * rows]
    theirs[...] = total[4 * rows :]


def join(mine, other, own, across, pair):
    rows = own.shape[0]
    total = mine[...] + other[...]
    own[...] = total[:rows]
    across[...] = total[rows : 2 * rows]
    pair[...] = total[2 * rows :]


def add_near(own, across, pair, total, passed):
    rows = own.shape[0]
    total[...] = (own[...] + across[...]) + pair[:rows]
    passed[...] = pair[rows:]


def add_up(columns, near, other, out):
    total = near[...] + other[...]
    for row in range(out.shape[0]):
        out[row] = total[row * columns : (row + 1) * columns]


SLOTS = 8


def announce(owners, _, out):
    for device in range(out.shape[0]):
        out[device] = owners[...]


def plan_rows(lines, everyone, _, plan, crowded):
    owner = everyone[:, 0, :]
    devices, width = owner.shape
    rows = plan.shape[1] // SLOTS
    lane = lax.broadcasted_iota(jnp.int32, owner.shape, 1)
    holder = jnp.where(lane < rows, jnp.floor(owner * (1.0 / lines)), -1.0)
    rank = jnp.zeros(owner.shape, F32)
    for row in range(rows):
        same = jnp.logical_and(holder == holder[:, row : row + 1], lane > row)
        rank = rank + jnp.where(same, 1.0, 0.0)
    most = jnp.max(jnp.where(lane < rows, rank, 0.0))
    crowded[0, 0] = jnp.where(most >= SLOTS, 1, 0).astype(jnp.int32)
    me = (lax.axis_index("cross") * 2 + lax.axis_index("elev")).astype(F32)
    columns = rows // lines
    place = (owner - holder * lines) * columns + (lane // lines).astype(F32) + 1.0
    place = jnp.where(holder == me, place, 0.0)
    slots = jnp.zeros(owner.shape, F32)
    for slot in range(SLOTS):
        found = jnp.sum(jnp.where(rank == slot, place, 0.0), axis=1, keepdims=True)
        slots = jnp.where(lane == slot, found, slots)
    slot_of = lax.broadcasted_iota(jnp.int32, (width, plan.shape[1]), 0)
    along = lax.broadcasted_iota(jnp.int32, (width, plan.shape[1]), 1)
    repeat = jnp.where(slot_of == lax.rem(along, SLOTS), 1.0, 0.0).astype(BF16)
    laid = times(slots.astype(BF16), repeat, False)
    device = lax.broadcasted_iota(jnp.int32, laid.shape, 0)
    wide = lax.broadcasted_iota(jnp.int32, laid.shape, 1)
    plan[...] = jnp.broadcast_to(
        jnp.sum(jnp.where(wide // SLOTS == device, laid, 0.0), axis=0, keepdims=True), plan.shape
    )


def place_rows(columns, plan, arrived, out):
    rows = out.shape[0] * columns
    values = arrived[...]
    high = values.astype(BF16)
    rest = values - high.astype(F32)
    middle = rest.astype(BF16)
    low = (rest - middle.astype(F32)).astype(BF16)
    wanted = lax.broadcasted_iota(jnp.int32, (rows, values.shape[0]), 0).astype(F32) + 1.0
    chosen = jnp.where(wanted == plan[:1], 1.0, 0.0).astype(BF16)
    total = times(chosen, high, False) + (times(chosen, middle, False) + times(chosen, low, False))
    for row in range(out.shape[0]):
        out[row] = total[row * columns : (row + 1) * columns]


def call(body, out_shape, in_specs, scratch=(), name=None, limit=16, out_specs=None):
    return pl.pallas_call(
        body,
        out_shape=out_shape,
        in_specs=in_specs,
        out_specs=jax.tree.map(lambda _: IN_VMEM, out_shape) if out_specs is None else out_specs,
        scratch_shapes=list(scratch),
        compiler_params=pltpu.CompilerParams(vmem_limit_bytes=limit * MIB),
        name=name,
    )


def shaped(shape, dtype=F32):
    return jax.ShapeDtypeStruct(shape, dtype)


def shards(source, pivot_inverse, coupling, skeleton_map, owners):
    lines, columns, size = source.shape
    depth = lax.axis_size("down")
    vectors = shaped((lines, size))
    every = shaped((columns, lines, size))
    stacked = shaped((lines, 2 * size, size), BF16)

    group = lax.axis_size(PLANE)
    rows = lines * columns
    targets = owners.T.reshape(1, rows)
    codes = (targets * columns + jnp.arange(rows, dtype=jnp.int32) // lines).astype(F32)
    codes = jnp.broadcast_to(jnp.tile(codes, (1, size // rows)), (8, size))
    holders = targets // lines
    before = jnp.arange(rows)[:, None] < jnp.arange(rows)[None, :]
    ranks = jnp.sum(jnp.logical_and(holders[0, :, None] == holders, before), axis=0, dtype=jnp.int32)
    slots = jnp.where(ranks < SLOTS, holders * SLOTS + ranks, -1).astype(F32)
    slots = jnp.broadcast_to(jnp.pad(slots, ((0, 0), (0, 128 - rows))), (8, 128))
    announced = jnp.broadcast_to(jnp.pad(targets.astype(F32), ((0, 0), (0, 128 - rows))), (8, 128))

    def dense(own, packed, plan):
        chips = lax.axis_size("cross")
        sides = 4

        def other_core(block):
            return lax.ppermute(block, "elev", [(0, 1), (1, 0)])

        def across_ring(block, stride):
            return lax.ppermute(block, "cross", [(chip, chip ^ 2 * stride) for chip in range(chips)])

        def beside_ring(block, stride):
            places = [(chip, core) for chip in range(chips) for core in range(2)]
            return lax.ppermute(
                block, PLANE, [(2 * chip + core, 2 * (chip ^ (1 + 2 * core) * stride) + core) for chip, core in places]
            )

        across = across_ring(own, 1)
        pair = beside_ring(jnp.concatenate([own, other_core(own)], axis=0), 1)
        quarter = shaped((rows, size))
        mine, theirs = call(
            functools.partial(gather_rows, lines, columns, sides),
            (shaped((4 * rows, size)),) * 2,
            [IN_VMEM] * 3,
            name="gather_rows",
        )(own, pair, across)
        own, across, pair = call(
            join, (quarter, quarter, shaped((2 * rows, size))), [IN_VMEM] * 2, name="join"
        )(mine, other_core(theirs))
        pair = beside_ring(pair, sides)
        across = across_ring(across, sides)
        near, passed = call(add_near, (quarter, quarter), [IN_VMEM] * 3, name="add_near")(own, across, pair)
        return call(
            functools.partial(add_up, columns), shaped(source.shape), [IN_VMEM] * 2, name="add_up"
        )(near, other_core(passed))

    def spread_out(own, packed, plan):
        moved = lax.all_to_all(packed.reshape(group, SLOTS, size), PLANE, 0, 0)
        return call(
            functools.partial(place_rows, columns), shaped(source.shape), [IN_VMEM] * 2, name="place_rows"
        )(plan, moved.reshape(group * SLOTS, size))

    matrices = pltpu.VMEM(pivot_inverse.shape, BF16)
    sent = call(
        first_sweep,
        vectors,
        [IN_HBM] * 3,
        [pltpu.VMEM(source.shape, F32), matrices, matrices, pltpu.SemaphoreType.DMA((2 * columns,))],
        name="first_sweep",
        limit=57,
    )(source, pivot_inverse, coupling)
    arrivals = []
    base = matrix = back = None

    def advance(place, *operands):
        return call(
            functools.partial(step, place), vectors, [IN_VMEM, IN_VMEM, IN_VMEM, ANYWHERE], name="step"
        )(*operands)

    for hop in range(1, depth):
        arrived = lax.ppermute(sent, "down", [(hop - 1, hop)])
        arrivals.append(arrived)
        if hop == 1:
            matrix, base = call(
                transfer,
                (stacked, vectors),
                [IN_VMEM, IN_HBM, IN_HBM],
                [
                    matrices,
                    matrices,
                    pltpu.VMEM((TOGETHER, columns - 1, size + EXTRA, size), F32),
                    pltpu.SemaphoreType.DMA((2, lines)),
                ],
                name="transfer",
                limit=49,
            )(source, pivot_inverse, coupling)
        if hop == 4:
            back = call(
                reverse_transfer, stacked, [IN_VMEM, IN_VMEM, ANYWHERE], name="reverse_transfer"
            )(pivot_inverse, coupling, sent)
        sent = advance(hop, arrived, matrix, base, base if back is None else back)
    forward, base = call(
        own_part, (every, vectors), [IN_VMEM] * 4 + [ANYWHERE], name="own_part"
    )(pivot_inverse, coupling, source, jnp.stack(arrivals), sent)
    arrivals = []
    everyone = None
    for hop in range(depth - 1, 0, -1):
        arrived = lax.ppermute(sent, "down", [(hop, hop - 1)])
        arrivals.append(arrived)
        if hop == 2:
            plan, crowded = call(
                functools.partial(plan_rows, lines),
                (shaped((8, group * SLOTS)), shaped((1, 1), jnp.int32)),
                [IN_VMEM, ANYWHERE],
                name="plan_rows",
                out_specs=(IN_VMEM, pl.BlockSpec(memory_space=pltpu.SMEM)),
            )(everyone, arrived)
        if hop == depth - 4:
            everyone = call(announce, shaped((group, 8, 128)), [IN_VMEM, ANYWHERE], name="announce")(announced, sent)
            everyone = lax.all_to_all(everyone, PLANE, 0, 0)
        if hop > 1:
            sent = advance(hop - 1, arrived, back, base, base if everyone is None else everyone)
    pressure, own, packed = call(
        finish,
        (shaped(source.shape), shaped((rows + 8, size)), shaped((group * SLOTS, size))),
        [IN_VMEM] * 7 + [ANYWHERE],
        name="finish",
    )(pivot_inverse, coupling, skeleton_map, codes, slots, forward, jnp.stack(arrivals), plan)
    forces = lax.cond(crowded[0, 0] == 0, spread_out, dense, own, packed, plan)
    return (pressure, forces)


def solution(mesh):
    in_specs = (
        P(PLANE, "down", None),
        P(PLANE, "down", None, None),
        P(PLANE, "down", None, None),
        P(PLANE, None, None),
        P(PLANE, "down"),
    )
    out_specs = (P(PLANE, "down", None), P(PLANE, "down", None))
    return jax.shard_map(shards, mesh=mesh, in_specs=in_specs, out_specs=out_specs, check_vma=False)
```

```python
import functools

import jax
import jax.numpy as jnp
from jax import lax
from jax.experimental import pallas as pl
from jax.experimental.pallas import tpu as pltpu
from jax.sharding import PartitionSpec as P

F32 = jnp.float32
BF16 = jnp.bfloat16
PLANE = ("cross", "elev")
MIB = 1024 * 1024
IN_VMEM = pl.BlockSpec(memory_space=pltpu.VMEM)
IN_HBM = pl.BlockSpec(memory_space=pltpu.HBM)
ANYWHERE = pl.BlockSpec(memory_space=pl.ANY)


def times(rows, matrix, transposed):
    return lax.dot_general(
        rows, matrix, (((1,), (1 if transposed else 0,)), ((), ())), preferred_element_type=F32
    )


def spread(vector):
    high = vector.astype(BF16).astype(F32)
    rest = vector - high
    middle = rest.astype(BF16).astype(F32)
    low = rest - middle
    parts = [high, middle, low]
    if vector.shape[0] % 16:
        parts.append(jnp.zeros_like(low))
    return jnp.concatenate(parts, axis=0).astype(BF16)


def per_line(vector, matrix_of, transposed, lines, twice=False):
    count = vector.shape[0]
    rows = spread(vector)
    if twice:
        rows = jnp.concatenate([rows, rows], axis=1)
    line_of = lax.rem(lax.broadcasted_iota(jnp.int32, vector.shape, 0), lines)
    total = jnp.zeros_like(vector)
    for line in range(lines):
        product = times(rows, matrix_of(line), transposed)
        product = product[:count] + product[count : 2 * count] + product[2 * count : 3 * count]
        total = jnp.where(line_of == line, product, total)
    return total


def halves(matrix):
    high = matrix.astype(BF16)
    low = (matrix - high.astype(F32)).astype(BF16)
    return jnp.concatenate([high, low], axis=1)


def product_of(pair, matrix, transposed):
    return times(pair, jnp.concatenate([matrix, matrix], axis=1 if transposed else 0), transposed)


def unit(size, sign=1.0):
    across = lax.broadcasted_iota(jnp.int32, (size, size), 0)
    along = lax.broadcasted_iota(jnp.int32, (size, size), 1)
    return jnp.where(across == along, sign, 0.0).astype(BF16)


def first_sweep(source_far, pivots, couple, leaving, source, pivots_here, couple_here, semaphores):
    lines, columns = source.shape[:2]

    @pl.when(lax.axis_index("down") == 0)
    def _():
        def fetch(column, far, near, kind):
            return pltpu.make_async_copy(far.at[:, column], near.at[:, column], semaphores.at[2 * column + kind])

        copies = [fetch(0, pivots, pivots_here, 1)]
        for column in range(1, columns):
            copies.append(fetch(column, couple, couple_here, 0))
            copies.append(fetch(column, pivots, pivots_here, 1))
        ahead = 4
        given_copy = pltpu.make_async_copy(source_far, source, semaphores.at[0])
        given_copy.start()
        for copy in copies[:ahead]:
            copy.start()
        given_copy.wait()

        def take(at):
            copies[at].wait()
            if at + ahead < len(copies):
                copies[at + ahead].start()

        carried = None
        for column in range(columns):
            given = source[:, column, :]
            if column:
                take(2 * column - 1)
                given = given - per_line(carried, lambda l: couple_here[l, column], True, lines)
            take(2 * column)
            carried = per_line(given, lambda l: pivots_here[l, column], True, lines)
        leaving[...] = carried


EXTRA = 16
TOGETHER = 4


def store_pair(matrix, line, pair):
    size = matrix.shape[2]
    matrix[line, :size] = pair[:, :size]
    matrix[line, size:] = pair[:, size:]


def forward_rows(source, pivots, couple, lines, keep=None):
    columns, size = pivots.shape[1], pivots.shape[2]
    blank = jnp.zeros((EXTRA - 1, size), F32)
    values = None
    for column in range(columns):
        given = []
        for at, line in enumerate(lines):
            own = jnp.concatenate([source[line, pl.ds(column, 1), :], blank], axis=0)
            if column:
                sent = product_of(halves(values[at]), couple[line, column], True)
                given.append(jnp.concatenate([-sent[:size], own - sent[size:]], axis=0))
            else:
                given.append(jnp.concatenate([-times(unit(size), couple[line, 0], True), own], axis=0))
        values = [product_of(halves(x), pivots[l, column], True) for x, l in zip(given, lines)]
        if keep is not None and column < columns - 1:
            for at, value in enumerate(values):
                keep[at, column] = value
    return values


def transfer(source, pivots_far, couple_far, matrix, base, pivots, couple, kept, semaphores):
    lines, columns = pivots.shape[:2]
    size = pivots.shape[2]
    here = lax.axis_index("down")
    last = lax.axis_size("down") - 1

    def fetch(line, act):
        for kind, (far, near) in enumerate(((couple_far, couple), (pivots_far, pivots))):
            act(pltpu.make_async_copy(far.at[line], near.at[line], semaphores.at[kind, line]))

    def arrive(some, first):
        for line in some:
            fetch(line, lambda copy: copy.wait())

        @pl.when(first + TOGETHER < lines)
        def _():
            for line in some:
                fetch(line + TOGETHER, lambda copy: copy.start())

    def hand_over(some, values):
        for line, value in zip(some, values):
            store_pair(matrix, line, halves(value[:size]))
            base[pl.ds(line, 1), :] = value[size : size + 1]

    @pl.when(here > 0)
    def _():
        for line in range(TOGETHER):
            fetch(line, lambda copy: copy.start())

    @pl.when(jnp.logical_and(here > 0, here < last))
    def _():
        @pl.loop(0, lines, step=TOGETHER)
        def _(first):
            some = [first + k for k in range(TOGETHER)]
            arrive(some, first)
            hand_over(some, forward_rows(source, pivots, couple, some))

    @pl.when(here == last)
    def _():
        @pl.loop(0, lines, step=TOGETHER)
        def _(first):
            some = [first + k for k in range(TOGETHER)]
            arrive(some, first)
            values = forward_rows(source, pivots, couple, some, kept)
            for column in range(columns - 1, -1, -1):
                values = [product_of(halves(x), couple[l, column], False) for x, l in zip(values, some)]
                if column:
                    values = [
                        kept[at, column - 1] - product_of(halves(x), pivots[l, column - 1], True)
                        for at, (x, l) in enumerate(zip(values, some))
                    ]
            hand_over(some, values)


def reverse_transfer(pivots, couple, _, matrix):
    lines, columns = pivots.shape[:2]
    size = pivots.shape[2]
    here = lax.axis_index("down")
    last = lax.axis_size("down") - 1

    @pl.when(jnp.logical_and(here > 0, here < last))
    def _():
        @pl.loop(0, lines, step=TOGETHER)
        def _(first):
            some = [first + k for k in range(TOGETHER)]
            pairs = [times(unit(size, -1.0), pivots[l, columns - 1], True).astype(BF16) for l in some]
            for column in range(columns - 1, -1, -1):
                if column == columns - 1:
                    values = [times(x, couple[l, column], False) for x, l in zip(pairs, some)]
                else:
                    values = [product_of(x, couple[l, column], False) for x, l in zip(pairs, some)]
                pairs = [halves(value) for value in values]
                if column:
                    pairs = [halves(-product_of(x, pivots[l, column - 1], True)) for x, l in zip(pairs, some)]
            for line, pair in zip(some, pairs):
                store_pair(matrix, line, pair)


def step(place, arrived, matrix, base, _, out):
    lines = base.shape[0]

    @pl.when(lax.axis_index("down") == place)
    def _():
        out[...] = base[...] + per_line(arrived[...], lambda l: matrix[l], False, lines, twice=True)


def own_part(pivots, couple, source, arrived, _, forward, base):
    lines, columns = pivots.shape[:2]
    carried = jnp.sum(arrived[...], axis=0)
    for column in range(columns):
        given = source[:, column, :] - per_line(carried, lambda l: couple[l, column], True, lines)
        carried = per_line(given, lambda l: pivots[l, column], True, lines)
        forward[column] = carried
    value = carried
    for column in range(columns - 1, -1, -1):
        carried = per_line(value, lambda l: couple[l, column], False, lines)
        if column:
            value = forward[column - 1] - per_line(carried, lambda l: pivots[l, column - 1], True, lines)
    base[...] = carried


def finish(pivots, couple, skeleton, codes, slots, forward, arrived, _, pressure, pushed, packed):
    lines, columns = pivots.shape[:2]
    carried = jnp.sum(arrived[...], axis=0)
    values = [None] * columns
    for column in range(columns - 1, -1, -1):
        value = forward[column] - per_line(carried, lambda l: pivots[l, column], True, lines)
        values[column] = value
        pressure[:, column, :] = value
        if column:
            carried = per_line(value, lambda l: couple[l, column], False, lines)
    rows = columns * lines
    force = per_line(jnp.concatenate(values, axis=0), lambda l: skeleton[l], True, lines)
    pushed[:rows] = force
    pushed[rows:] = codes[...]
    slot = lax.broadcasted_iota(jnp.int32, (packed.shape[0], rows), 0).astype(F32)
    chosen = jnp.where(slot == slots[:1, :rows], 1.0, 0.0).astype(BF16)
    parts = spread(force)
    packed[...] = times(chosen, parts[:rows], False) + (
        times(chosen, parts[rows : 2 * rows], False) + times(chosen, parts[2 * rows :], False)
    )


def gather_rows(lines, columns, sides, own, pair, across, mine, theirs):
    rows = lines * columns
    chip, core = lax.axis_index("cross"), lax.axis_index("elev")
    height = own.shape[0]
    blocks = [own[...], pair[:height], pair[height:], across[...]]
    block_of = lax.broadcasted_iota(jnp.int32, (1, len(blocks) * rows), 1) // rows
    codes = jnp.zeros(block_of.shape, F32)
    for at, block in enumerate(blocks):
        codes = jnp.where(block_of == at, block[rows : rows + 1, : len(blocks) * rows], codes)
    values = jnp.concatenate([block[:rows] for block in blocks], axis=0)
    high = values.astype(BF16)
    rest = values - high.astype(F32)
    middle = rest.astype(BF16)
    low = (rest - middle.astype(F32)).astype(BF16)
    here = lax.broadcasted_iota(jnp.int32, (rows, 1), 0)
    wanted = []
    for turn in range(2):
        holder = core if turn == 0 else 1 - core
        beside = 1 + 2 * holder
        for way, owner in ((0, holder), (2, holder), (beside, holder), (beside, 1 - holder)):
            target = (chip // sides ^ way) * sides + lax.rem(chip, sides)
            wanted.append((target * 2 + owner) * rows + here)
    wanted = jnp.concatenate(wanted, axis=0).astype(F32)
    chosen = jnp.where(wanted == codes, 1.0, 0.0).astype(BF16)
    total = times(chosen, high, False) + (times(chosen, middle, False) + times(chosen, low, False))
    mine[...] = total[: 4 * rows]
    theirs[...] = total[4 * rows :]


def join(mine, other, own, across, pair):
    rows = own.shape[0]
    total = mine[...] + other[...]
    own[...] = total[:rows]
    across[...] = total[rows : 2 * rows]
    pair[...] = total[2 * rows :]


def add_near(own, across, pair, total, passed):
    rows = own.shape[0]
    total[...] = (own[...] + across[...]) + pair[:rows]
    passed[...] = pair[rows:]


def add_up(columns, near, other, out):
    total = near[...] + other[...]
    for row in range(out.shape[0]):
        out[row] = total[row * columns : (row + 1) * columns]


SLOTS = 8


def announce(owners, _, out):
    for device in range(out.shape[0]):
        out[device] = owners[...]


def plan_rows(lines, everyone, *refs):
    plan, crowded = refs[-2:]
    owner = everyone[:, 0, :]
    devices, width = owner.shape
    rows = plan.shape[1] // SLOTS
    lane = lax.broadcasted_iota(jnp.int32, owner.shape, 1)
    holder = jnp.where(lane < rows, jnp.floor(owner * (1.0 / lines)), -1.0)
    rank = jnp.zeros(owner.shape, F32)
    for row in range(rows):
        same = jnp.logical_and(holder == holder[:, row : row + 1], lane > row)
        rank = rank + jnp.where(same, 1.0, 0.0)
    most = jnp.max(jnp.where(lane < rows, rank, 0.0))
    crowded[0, 0] = jnp.where(most >= SLOTS, 1, 0).astype(jnp.int32)
    me = (lax.axis_index("cross") * 2 + lax.axis_index("elev")).astype(F32)
    columns = rows // lines
    place = (owner - holder * lines) * columns + (lane // lines).astype(F32) + 1.0
    place = jnp.where(holder == me, place, 0.0)
    slots = jnp.zeros(owner.shape, F32)
    for slot in range(SLOTS):
        found = jnp.sum(jnp.where(rank == slot, place, 0.0), axis=1, keepdims=True)
        slots = jnp.where(lane == slot, found, slots)
    slot_of = lax.broadcasted_iota(jnp.int32, (width, plan.shape[1]), 0)
    along = lax.broadcasted_iota(jnp.int32, (width, plan.shape[1]), 1)
    repeat = jnp.where(slot_of == lax.rem(along, SLOTS), 1.0, 0.0).astype(BF16)
    laid = times(slots.astype(BF16), repeat, False)
    device = lax.broadcasted_iota(jnp.int32, laid.shape, 0)
    wide = lax.broadcasted_iota(jnp.int32, laid.shape, 1)
    plan[...] = jnp.broadcast_to(
        jnp.sum(jnp.where(wide // SLOTS == device, laid, 0.0), axis=0, keepdims=True), plan.shape
    )


def place_rows(columns, plan, arrived, out):
    rows = out.shape[0] * columns
    values = arrived[...]
    high = values.astype(BF16)
    rest = values - high.astype(F32)
    middle = rest.astype(BF16)
    low = (rest - middle.astype(F32)).astype(BF16)
    wanted = lax.broadcasted_iota(jnp.int32, (rows, values.shape[0]), 0).astype(F32) + 1.0
    chosen = jnp.where(wanted == plan[:1], 1.0, 0.0).astype(BF16)
    total = times(chosen, high, False) + (times(chosen, middle, False) + times(chosen, low, False))
    for row in range(out.shape[0]):
        out[row] = total[row * columns : (row + 1) * columns]


def call(body, out_shape, in_specs, scratch=(), name=None, limit=16, out_specs=None):
    return pl.pallas_call(
        body,
        out_shape=out_shape,
        in_specs=in_specs,
        out_specs=jax.tree.map(lambda _: IN_VMEM, out_shape) if out_specs is None else out_specs,
        scratch_shapes=list(scratch),
        compiler_params=pltpu.CompilerParams(vmem_limit_bytes=limit * MIB),
        name=name,
    )


def shaped(shape, dtype=F32):
    return jax.ShapeDtypeStruct(shape, dtype)


def shards(source, pivot_inverse, coupling, skeleton_map, owners):
    lines, columns, size = source.shape
    depth = lax.axis_size("down")
    vectors = shaped((lines, size))
    every = shaped((columns, lines, size))
    stacked = shaped((lines, 2 * size, size), BF16)

    group = lax.axis_size(PLANE)
    rows = lines * columns
    targets = owners.T.reshape(1, rows)
    codes = (targets * columns + jnp.arange(rows, dtype=jnp.int32) // lines).astype(F32)
    codes = jnp.broadcast_to(jnp.tile(codes, (1, size // rows)), (8, size))
    holders = targets // lines
    before = jnp.arange(rows)[:, None] < jnp.arange(rows)[None, :]
    ranks = jnp.sum(jnp.logical_and(holders[0, :, None] == holders, before), axis=0, dtype=jnp.int32)
    slots = jnp.where(ranks < SLOTS, holders * SLOTS + ranks, -1).astype(F32)
    slots = jnp.broadcast_to(jnp.pad(slots, ((0, 0), (0, 128 - rows))), (8, 128))
    announced = jnp.broadcast_to(jnp.pad(targets.astype(F32), ((0, 0), (0, 128 - rows))), (8, 128))

    def dense(own, packed, plan):
        chips = lax.axis_size("cross")
        sides = 4

        def other_core(block):
            return lax.ppermute(block, "elev", [(0, 1), (1, 0)])

        def across_ring(block, stride):
            return lax.ppermute(block, "cross", [(chip, chip ^ 2 * stride) for chip in range(chips)])

        def beside_ring(block, stride):
            places = [(chip, core) for chip in range(chips) for core in range(2)]
            return lax.ppermute(
                block, PLANE, [(2 * chip + core, 2 * (chip ^ (1 + 2 * core) * stride) + core) for chip, core in places]
            )

        across = across_ring(own, 1)
        pair = beside_ring(jnp.concatenate([own, other_core(own)], axis=0), 1)
        quarter = shaped((rows, size))
        mine, theirs = call(
            functools.partial(gather_rows, lines, columns, sides),
            (shaped((4 * rows, size)),) * 2,
            [IN_VMEM] * 3,
            name="gather_rows",
        )(own, pair, across)
        own, across, pair = call(
            join, (quarter, quarter, shaped((2 * rows, size))), [IN_VMEM] * 2, name="join"
        )(mine, other_core(theirs))
        pair = beside_ring(pair, sides)
        across = across_ring(across, sides)
        near, passed = call(add_near, (quarter, quarter), [IN_VMEM] * 3, name="add_near")(own, across, pair)
        return call(
            functools.partial(add_up, columns), shaped(source.shape), [IN_VMEM] * 2, name="add_up"
        )(near, other_core(passed))

    def spread_out(own, packed, plan):
        moved = lax.all_to_all(packed.reshape(group, SLOTS, size), PLANE, 0, 0)
        return call(
            functools.partial(place_rows, columns), shaped(source.shape), [IN_VMEM] * 2, name="place_rows"
        )(plan, moved.reshape(group * SLOTS, size))

    matrices = pltpu.VMEM(pivot_inverse.shape, BF16)
    sent = call(
        first_sweep,
        vectors,
        [IN_HBM] * 3,
        [pltpu.VMEM(source.shape, F32), matrices, matrices, pltpu.SemaphoreType.DMA((2 * columns,))],
        name="first_sweep",
        limit=57,
    )(source, pivot_inverse, coupling)
    arrivals = []
    base = matrix = back = None

    def advance(place, *operands):
        return call(
            functools.partial(step, place), vectors, [IN_VMEM, IN_VMEM, IN_VMEM, ANYWHERE], name="step"
        )(*operands)

    for hop in range(1, depth):
        arrived = lax.ppermute(sent, "down", [(hop - 1, hop)])
        arrivals.append(arrived)
        if hop == 1:
            matrix, base = call(
                transfer,
                (stacked, vectors),
                [IN_VMEM, IN_HBM, IN_HBM],
                [
                    matrices,
                    matrices,
                    pltpu.VMEM((TOGETHER, columns - 1, size + EXTRA, size), F32),
                    pltpu.SemaphoreType.DMA((2, lines)),
                ],
                name="transfer",
                limit=49,
            )(source, pivot_inverse, coupling)
        if hop == 4:
            back = call(
                reverse_transfer, stacked, [IN_VMEM, IN_VMEM, ANYWHERE], name="reverse_transfer"
            )(pivot_inverse, coupling, sent)
        sent = advance(hop, arrived, matrix, base, base if back is None else back)
    forward, base = call(
        own_part, (every, vectors), [IN_VMEM] * 4 + [ANYWHERE], name="own_part"
    )(pivot_inverse, coupling, source, jnp.stack(arrivals), sent)
    arrivals = []
    everyone = None
    for hop in range(depth - 1, 0, -1):
        arrived = lax.ppermute(sent, "down", [(hop, hop - 1)])
        arrivals.append(arrived)
        if hop == 3:
            plan, crowded = call(
                functools.partial(plan_rows, lines),
                (shaped((8, group * SLOTS)), shaped((1, 1), jnp.int32)),
                [IN_VMEM] * 4 + [ANYWHERE],
                name="plan_rows",
                out_specs=(IN_VMEM, pl.BlockSpec(memory_space=pltpu.SMEM)),
            )(everyone, pivot_inverse, coupling, skeleton_map, arrived)
        if hop == depth - 4:
            everyone = call(announce, shaped((group, 8, 128)), [IN_VMEM, ANYWHERE], name="announce")(announced, sent)
            everyone = lax.all_to_all(everyone, PLANE, 0, 0)
        if hop > 1:
            ready = base if everyone is None else everyone if hop > 2 else plan
            sent = advance(hop - 1, arrived, back, base, ready)
    pressure, own, packed = call(
        finish,
        (shaped(source.shape), shaped((rows + 8, size)), shaped((group * SLOTS, size))),
        [IN_VMEM] * 7 + [ANYWHERE],
        name="finish",
    )(pivot_inverse, coupling, skeleton_map, codes, slots, forward, jnp.stack(arrivals), plan)
    forces = lax.cond(crowded[0, 0] == 0, spread_out, dense, own, packed, plan)
    return (pressure, forces)


def solution(mesh):
    in_specs = (
        P(PLANE, "down", None),
        P(PLANE, "down", None, None),
        P(PLANE, "down", None, None),
        P(PLANE, None, None),
        P(PLANE, "down"),
    )
    out_specs = (P(PLANE, "down", None), P(PLANE, "down", None))
    return jax.shard_map(shards, mesh=mesh, in_specs=in_specs, out_specs=out_specs, check_vma=False)
```

```python
import functools

import jax
import jax.numpy as jnp
from jax import lax
from jax.experimental import pallas as pl
from jax.experimental.pallas import tpu as pltpu
from jax.sharding import PartitionSpec as P

F32 = jnp.float32
BF16 = jnp.bfloat16
PLANE = ("cross", "elev")
MIB = 1024 * 1024
IN_VMEM = pl.BlockSpec(memory_space=pltpu.VMEM)
IN_HBM = pl.BlockSpec(memory_space=pltpu.HBM)
ANYWHERE = pl.BlockSpec(memory_space=pl.ANY)


def times(rows, matrix, transposed):
    return lax.dot_general(
        rows, matrix, (((1,), (1 if transposed else 0,)), ((), ())), preferred_element_type=F32
    )


def spread(vector):
    high = vector.astype(BF16).astype(F32)
    rest = vector - high
    middle = rest.astype(BF16).astype(F32)
    low = rest - middle
    parts = [high, middle, low]
    if vector.shape[0] % 16:
        parts.append(jnp.zeros_like(low))
    return jnp.concatenate(parts, axis=0).astype(BF16)


def per_line(vector, matrix_of, transposed, lines, twice=False):
    count = vector.shape[0]
    rows = spread(vector)
    if twice:
        rows = jnp.concatenate([rows, rows], axis=1)
    line_of = lax.rem(lax.broadcasted_iota(jnp.int32, vector.shape, 0), lines)
    total = jnp.zeros_like(vector)
    for line in range(lines):
        product = times(rows, matrix_of(line), transposed)
        product = product[:count] + product[count : 2 * count] + product[2 * count : 3 * count]
        total = jnp.where(line_of == line, product, total)
    return total


def halves(matrix):
    high = matrix.astype(BF16)
    low = (matrix - high.astype(F32)).astype(BF16)
    return jnp.concatenate([high, low], axis=1)


def product_of(pair, matrix, transposed):
    return times(pair, jnp.concatenate([matrix, matrix], axis=1 if transposed else 0), transposed)


def unit(size, sign=1.0):
    across = lax.broadcasted_iota(jnp.int32, (size, size), 0)
    along = lax.broadcasted_iota(jnp.int32, (size, size), 1)
    return jnp.where(across == along, sign, 0.0).astype(BF16)


def first_sweep(source_far, pivots, couple, leaving, source, pivots_here, couple_here, semaphores):
    lines, columns = source.shape[:2]

    @pl.when(lax.axis_index("down") == 0)
    def _():
        def fetch(column, far, near, kind):
            return pltpu.make_async_copy(far.at[:, column], near.at[:, column], semaphores.at[2 * column + kind])

        copies = [fetch(0, pivots, pivots_here, 1)]
        for column in range(1, columns):
            copies.append(fetch(column, couple, couple_here, 0))
            copies.append(fetch(column, pivots, pivots_here, 1))
        ahead = 4
        given_copy = pltpu.make_async_copy(source_far, source, semaphores.at[0])
        given_copy.start()
        for copy in copies[:ahead]:
            copy.start()
        given_copy.wait()

        def take(at):
            copies[at].wait()
            if at + ahead < len(copies):
                copies[at + ahead].start()

        carried = None
        for column in range(columns):
            given = source[:, column, :]
            if column:
                take(2 * column - 1)
                given = given - per_line(carried, lambda l: couple_here[l, column], True, lines)
            take(2 * column)
            carried = per_line(given, lambda l: pivots_here[l, column], True, lines)
        leaving[...] = carried


EXTRA = 16
TOGETHER = 4


def store_pair(matrix, line, pair):
    size = matrix.shape[2]
    matrix[line, :size] = pair[:, :size]
    matrix[line, size:] = pair[:, size:]


def forward_rows(source, pivots, couple, lines, keep=None):
    columns, size = pivots.shape[1], pivots.shape[2]
    blank = jnp.zeros((EXTRA - 1, size), F32)
    values = None
    for column in range(columns):
        given = []
        for at, line in enumerate(lines):
            own = jnp.concatenate([source[line, pl.ds(column, 1), :], blank], axis=0)
            if column:
                sent = product_of(halves(values[at]), couple[line, column], True)
                given.append(jnp.concatenate([-sent[:size], own - sent[size:]], axis=0))
            else:
                given.append(jnp.concatenate([-times(unit(size), couple[line, 0], True), own], axis=0))
        values = [product_of(halves(x), pivots[l, column], True) for x, l in zip(given, lines)]
        if keep is not None and column < columns - 1:
            for at, value in enumerate(values):
                keep[at, column] = value
    return values


def transfer(early, source, pivots_far, couple_far, _, matrix, base, pivots, couple, kept, semaphores):
    lines, columns = pivots.shape[:2]
    size = pivots.shape[2]
    here = lax.axis_index("down")
    last = lax.axis_size("down") - 1

    def fetch(line, act):
        for kind, (far, near) in enumerate(((couple_far, couple), (pivots_far, pivots))):
            act(pltpu.make_async_copy(far.at[line], near.at[line], semaphores.at[kind, line]))

    def arrive(some, first):
        for line in some:
            fetch(line, lambda copy: copy.wait())

        @pl.when(first + TOGETHER < lines)
        def _():
            for line in some:
                fetch(line + TOGETHER, lambda copy: copy.start())

    def hand_over(some, values):
        for line, value in zip(some, values):
            store_pair(matrix, line, halves(value[:size]))
            base[pl.ds(line, 1), :] = value[size : size + 1]

    active = here == 1 if early else here > 1

    @pl.when(active)
    def _():
        for line in range(TOGETHER):
            fetch(line, lambda copy: copy.start())

    @pl.when(jnp.logical_and(active, here < last))
    def _():
        @pl.loop(0, lines, step=TOGETHER)
        def _(first):
            some = [first + k for k in range(TOGETHER)]
            arrive(some, first)
            hand_over(some, forward_rows(source, pivots, couple, some))

    @pl.when(jnp.logical_and(active, here == last))
    def _():
        @pl.loop(0, lines, step=TOGETHER)
        def _(first):
            some = [first + k for k in range(TOGETHER)]
            arrive(some, first)
            values = forward_rows(source, pivots, couple, some, kept)
            for column in range(columns - 1, -1, -1):
                values = [product_of(halves(x), couple[l, column], False) for x, l in zip(values, some)]
                if column:
                    values = [
                        kept[at, column - 1] - product_of(halves(x), pivots[l, column - 1], True)
                        for at, (x, l) in enumerate(zip(values, some))
                    ]
            hand_over(some, values)


def reverse_transfer(pivots, couple, _, matrix):
    lines, columns = pivots.shape[:2]
    size = pivots.shape[2]
    here = lax.axis_index("down")
    last = lax.axis_size("down") - 1

    @pl.when(jnp.logical_and(here > 0, here < last))
    def _():
        @pl.loop(0, lines, step=TOGETHER)
        def _(first):
            some = [first + k for k in range(TOGETHER)]
            pairs = [times(unit(size, -1.0), pivots[l, columns - 1], True).astype(BF16) for l in some]
            for column in range(columns - 1, -1, -1):
                if column == columns - 1:
                    values = [times(x, couple[l, column], False) for x, l in zip(pairs, some)]
                else:
                    values = [product_of(x, couple[l, column], False) for x, l in zip(pairs, some)]
                pairs = [halves(value) for value in values]
                if column:
                    pairs = [halves(-product_of(x, pivots[l, column - 1], True)) for x, l in zip(pairs, some)]
            for line, pair in zip(some, pairs):
                store_pair(matrix, line, pair)


def step(place, arrived, matrix, base, _, out):
    lines = base.shape[0]

    @pl.when(lax.axis_index("down") == place)
    def _():
        out[...] = base[...] + per_line(arrived[...], lambda l: matrix[l], False, lines, twice=True)


def own_part(pivots, couple, source, arrived, _, forward, base):
    lines, columns = pivots.shape[:2]
    carried = jnp.sum(arrived[...], axis=0)
    for column in range(columns):
        given = source[:, column, :] - per_line(carried, lambda l: couple[l, column], True, lines)
        carried = per_line(given, lambda l: pivots[l, column], True, lines)
        forward[column] = carried
    value = carried
    for column in range(columns - 1, -1, -1):
        carried = per_line(value, lambda l: couple[l, column], False, lines)
        if column:
            value = forward[column - 1] - per_line(carried, lambda l: pivots[l, column - 1], True, lines)
    base[...] = carried


def finish(pivots, couple, skeleton, codes, slots, forward, arrived, _, pressure, pushed, packed):
    lines, columns = pivots.shape[:2]
    carried = jnp.sum(arrived[...], axis=0)
    values = [None] * columns
    for column in range(columns - 1, -1, -1):
        value = forward[column] - per_line(carried, lambda l: pivots[l, column], True, lines)
        values[column] = value
        pressure[:, column, :] = value
        if column:
            carried = per_line(value, lambda l: couple[l, column], False, lines)
    rows = columns * lines
    force = per_line(jnp.concatenate(values, axis=0), lambda l: skeleton[l], True, lines)
    pushed[:rows] = force
    pushed[rows:] = codes[...]
    slot = lax.broadcasted_iota(jnp.int32, (packed.shape[0], rows), 0).astype(F32)
    chosen = jnp.where(slot == slots[:1, :rows], 1.0, 0.0).astype(BF16)
    parts = spread(force)
    packed[...] = times(chosen, parts[:rows], False) + (
        times(chosen, parts[rows : 2 * rows], False) + times(chosen, parts[2 * rows :], False)
    )


def gather_rows(lines, columns, sides, own, pair, across, mine, theirs):
    rows = lines * columns
    chip, core = lax.axis_index("cross"), lax.axis_index("elev")
    height = own.shape[0]
    blocks = [own[...], pair[:height], pair[height:], across[...]]
    block_of = lax.broadcasted_iota(jnp.int32, (1, len(blocks) * rows), 1) // rows
    codes = jnp.zeros(block_of.shape, F32)
    for at, block in enumerate(blocks):
        codes = jnp.where(block_of == at, block[rows : rows + 1, : len(blocks) * rows], codes)
    values = jnp.concatenate([block[:rows] for block in blocks], axis=0)
    high = values.astype(BF16)
    rest = values - high.astype(F32)
    middle = rest.astype(BF16)
    low = (rest - middle.astype(F32)).astype(BF16)
    here = lax.broadcasted_iota(jnp.int32, (rows, 1), 0)
    wanted = []
    for turn in range(2):
        holder = core if turn == 0 else 1 - core
        beside = 1 + 2 * holder
        for way, owner in ((0, holder), (2, holder), (beside, holder), (beside, 1 - holder)):
            target = (chip // sides ^ way) * sides + lax.rem(chip, sides)
            wanted.append((target * 2 + owner) * rows + here)
    wanted = jnp.concatenate(wanted, axis=0).astype(F32)
    chosen = jnp.where(wanted == codes, 1.0, 0.0).astype(BF16)
    total = times(chosen, high, False) + (times(chosen, middle, False) + times(chosen, low, False))
    mine[...] = total[: 4 * rows]
    theirs[...] = total[4 * rows :]


def join(mine, other, own, across, pair):
    rows = own.shape[0]
    total = mine[...] + other[...]
    own[...] = total[:rows]
    across[...] = total[rows : 2 * rows]
    pair[...] = total[2 * rows :]


def add_near(own, across, pair, total, passed):
    rows = own.shape[0]
    total[...] = (own[...] + across[...]) + pair[:rows]
    passed[...] = pair[rows:]


def add_up(columns, near, other, out):
    total = near[...] + other[...]
    for row in range(out.shape[0]):
        out[row] = total[row * columns : (row + 1) * columns]


SLOTS = 8


def announce(owners, _, out):
    for device in range(out.shape[0]):
        out[device] = owners[...]


def plan_rows(lines, everyone, *refs):
    plan, crowded = refs[-2:]
    owner = everyone[:, 0, :]
    devices, width = owner.shape
    rows = plan.shape[1] // SLOTS
    lane = lax.broadcasted_iota(jnp.int32, owner.shape, 1)
    holder = jnp.where(lane < rows, jnp.floor(owner * (1.0 / lines)), -1.0)
    rank = jnp.zeros(owner.shape, F32)
    for row in range(rows):
        same = jnp.logical_and(holder == holder[:, row : row + 1], lane > row)
        rank = rank + jnp.where(same, 1.0, 0.0)
    most = jnp.max(jnp.where(lane < rows, rank, 0.0))
    crowded[0, 0] = jnp.where(most >= SLOTS, 1, 0).astype(jnp.int32)
    me = (lax.axis_index("cross") * 2 + lax.axis_index("elev")).astype(F32)
    columns = rows // lines
    place = (owner - holder * lines) * columns + (lane // lines).astype(F32) + 1.0
    place = jnp.where(holder == me, place, 0.0)
    slots = jnp.zeros(owner.shape, F32)
    for slot in range(SLOTS):
        found = jnp.sum(jnp.where(rank == slot, place, 0.0), axis=1, keepdims=True)
        slots = jnp.where(lane == slot, found, slots)
    slot_of = lax.broadcasted_iota(jnp.int32, (width, plan.shape[1]), 0)
    along = lax.broadcasted_iota(jnp.int32, (width, plan.shape[1]), 1)
    repeat = jnp.where(slot_of == lax.rem(along, SLOTS), 1.0, 0.0).astype(BF16)
    laid = times(slots.astype(BF16), repeat, False)
    device = lax.broadcasted_iota(jnp.int32, laid.shape, 0)
    wide = lax.broadcasted_iota(jnp.int32, laid.shape, 1)
    plan[...] = jnp.broadcast_to(
        jnp.sum(jnp.where(wide // SLOTS == device, laid, 0.0), axis=0, keepdims=True), plan.shape
    )


def place_rows(columns, plan, arrived, out):
    rows = out.shape[0] * columns
    values = arrived[...]
    high = values.astype(BF16)
    rest = values - high.astype(F32)
    middle = rest.astype(BF16)
    low = (rest - middle.astype(F32)).astype(BF16)
    wanted = lax.broadcasted_iota(jnp.int32, (rows, values.shape[0]), 0).astype(F32) + 1.0
    chosen = jnp.where(wanted == plan[:1], 1.0, 0.0).astype(BF16)
    total = times(chosen, high, False) + (times(chosen, middle, False) + times(chosen, low, False))
    for row in range(out.shape[0]):
        out[row] = total[row * columns : (row + 1) * columns]


def call(body, out_shape, in_specs, scratch=(), name=None, limit=16, out_specs=None):
    return pl.pallas_call(
        body,
        out_shape=out_shape,
        in_specs=in_specs,
        out_specs=jax.tree.map(lambda _: IN_VMEM, out_shape) if out_specs is None else out_specs,
        scratch_shapes=list(scratch),
        compiler_params=pltpu.CompilerParams(vmem_limit_bytes=limit * MIB),
        name=name,
    )


def shaped(shape, dtype=F32):
    return jax.ShapeDtypeStruct(shape, dtype)


def shards(source, pivot_inverse, coupling, skeleton_map, owners):
    lines, columns, size = source.shape
    depth = lax.axis_size("down")
    vectors = shaped((lines, size))
    every = shaped((columns, lines, size))
    stacked = shaped((lines, 2 * size, size), BF16)

    group = lax.axis_size(PLANE)
    rows = lines * columns
    targets = owners.T.reshape(1, rows)
    codes = (targets * columns + jnp.arange(rows, dtype=jnp.int32) // lines).astype(F32)
    codes = jnp.broadcast_to(jnp.tile(codes, (1, size // rows)), (8, size))
    holders = targets // lines
    before = jnp.arange(rows)[:, None] < jnp.arange(rows)[None, :]
    ranks = jnp.sum(jnp.logical_and(holders[0, :, None] == holders, before), axis=0, dtype=jnp.int32)
    slots = jnp.where(ranks < SLOTS, holders * SLOTS + ranks, -1).astype(F32)
    slots = jnp.broadcast_to(jnp.pad(slots, ((0, 0), (0, 128 - rows))), (8, 128))
    announced = jnp.broadcast_to(jnp.pad(targets.astype(F32), ((0, 0), (0, 128 - rows))), (8, 128))

    def dense(own, packed, plan):
        chips = lax.axis_size("cross")
        sides = 4

        def other_core(block):
            return lax.ppermute(block, "elev", [(0, 1), (1, 0)])

        def across_ring(block, stride):
            return lax.ppermute(block, "cross", [(chip, chip ^ 2 * stride) for chip in range(chips)])

        def beside_ring(block, stride):
            places = [(chip, core) for chip in range(chips) for core in range(2)]
            return lax.ppermute(
                block, PLANE, [(2 * chip + core, 2 * (chip ^ (1 + 2 * core) * stride) + core) for chip, core in places]
            )

        across = across_ring(own, 1)
        pair = beside_ring(jnp.concatenate([own, other_core(own)], axis=0), 1)
        quarter = shaped((rows, size))
        mine, theirs = call(
            functools.partial(gather_rows, lines, columns, sides),
            (shaped((4 * rows, size)),) * 2,
            [IN_VMEM] * 3,
            name="gather_rows",
        )(own, pair, across)
        own, across, pair = call(
            join, (quarter, quarter, shaped((2 * rows, size))), [IN_VMEM] * 2, name="join"
        )(mine, other_core(theirs))
        pair = beside_ring(pair, sides)
        across = across_ring(across, sides)
        near, passed = call(add_near, (quarter, quarter), [IN_VMEM] * 3, name="add_near")(own, across, pair)
        return call(
            functools.partial(add_up, columns), shaped(source.shape), [IN_VMEM] * 2, name="add_up"
        )(near, other_core(passed))

    def spread_out(own, packed, plan):
        moved = lax.all_to_all(packed.reshape(group, SLOTS, size), PLANE, 0, 0)
        return call(
            functools.partial(place_rows, columns), shaped(source.shape), [IN_VMEM] * 2, name="place_rows"
        )(plan, moved.reshape(group * SLOTS, size))

    matrices = pltpu.VMEM(pivot_inverse.shape, BF16)
    sent = call(
        first_sweep,
        vectors,
        [IN_HBM] * 3,
        [pltpu.VMEM(source.shape, F32), matrices, matrices, pltpu.SemaphoreType.DMA((2 * columns,))],
        name="first_sweep",
        limit=57,
    )(source, pivot_inverse, coupling)
    arrivals = []
    base = matrix = back = None

    def advance(place, *operands):
        return call(
            functools.partial(step, place), vectors, [IN_VMEM, IN_VMEM, IN_VMEM, ANYWHERE], name="step"
        )(*operands)

    for hop in range(1, depth):
        arrived = lax.ppermute(sent, "down", [(hop - 1, hop)])
        arrivals.append(arrived)
        if hop <= 2:
            matrix, base = call(
                functools.partial(transfer, hop == 1),
                (stacked, vectors),
                [IN_VMEM, IN_HBM, IN_HBM, ANYWHERE],
                [
                    matrices,
                    matrices,
                    pltpu.VMEM((TOGETHER, columns - 1, size + EXTRA, size), F32),
                    pltpu.SemaphoreType.DMA((2, lines)),
                ],
                name="transfer",
                limit=49,
            )(source, pivot_inverse, coupling, coupling if hop == 1 else sent)
        if hop == 4:
            back = call(
                reverse_transfer, stacked, [IN_VMEM, IN_VMEM, ANYWHERE], name="reverse_transfer"
            )(pivot_inverse, coupling, sent)
        sent = advance(hop, arrived, matrix, base, base if back is None else back)
    forward, base = call(
        own_part, (every, vectors), [IN_VMEM] * 4 + [ANYWHERE], name="own_part"
    )(pivot_inverse, coupling, source, jnp.stack(arrivals), sent)
    arrivals = []
    everyone = None
    for hop in range(depth - 1, 0, -1):
        arrived = lax.ppermute(sent, "down", [(hop, hop - 1)])
        arrivals.append(arrived)
        if hop == 3:
            plan, crowded = call(
                functools.partial(plan_rows, lines),
                (shaped((8, group * SLOTS)), shaped((1, 1), jnp.int32)),
                [IN_VMEM] * 4 + [ANYWHERE],
                name="plan_rows",
                out_specs=(IN_VMEM, pl.BlockSpec(memory_space=pltpu.SMEM)),
            )(everyone, pivot_inverse, coupling, skeleton_map, arrived)
        if hop == depth - 4:
            everyone = call(announce, shaped((group, 8, 128)), [IN_VMEM, ANYWHERE], name="announce")(announced, sent)
            everyone = lax.all_to_all(everyone, PLANE, 0, 0)
        if hop > 1:
            ready = base if everyone is None else everyone if hop > 2 else plan
            sent = advance(hop - 1, arrived, back, base, ready)
    pressure, own, packed = call(
        finish,
        (shaped(source.shape), shaped((rows + 8, size)), shaped((group * SLOTS, size))),
        [IN_VMEM] * 7 + [ANYWHERE],
        name="finish",
    )(pivot_inverse, coupling, skeleton_map, codes, slots, forward, jnp.stack(arrivals), plan)
    forces = lax.cond(crowded[0, 0] == 0, spread_out, dense, own, packed, plan)
    return (pressure, forces)


def solution(mesh):
    in_specs = (
        P(PLANE, "down", None),
        P(PLANE, "down", None, None),
        P(PLANE, "down", None, None),
        P(PLANE, None, None),
        P(PLANE, "down"),
    )
    out_specs = (P(PLANE, "down", None), P(PLANE, "down", None))
    return jax.shard_map(shards, mesh=mesh, in_specs=in_specs, out_specs=out_specs, check_vma=False)
```
